32 devices in a mesh: face: 4 (over z), elem: 8 (over y, x, core).
Axes of the slice: x: 2, y: 2, z: 4, core: 2. Of those that a mesh axis runs over, the one named last changes fastest.
Arguments:
- tracers: float32 [4, 72, 64, 1024], P(None, None, 'face', 'elem'), may hold values from 0 to 2
- thickness: float32 [72, 64, 1024], P(None, 'face', 'elem'), may hold values from 0.5 to 1.5
- winds: float32 [2, 72, 64, 1024], P(None, None, 'face', 'elem'), may hold values from -4 to 4
- wave_coef: float32 [72], replicated, may hold values from 0.02 to 0.12
- depart: int32 [16, 256], P('face', 'elem'), may hold values from 0 to 4095, as said below
- offsets: int32 [2, 64, 1024], P(None, 'face', 'elem'), may hold values from 0 to 63
Outputs:
- tracer_mass: float32 [4, 72, 64, 1024], P(None, None, 'face', 'elem')
- new_height: float32 [72, 64, 1024], P(None, 'face', 'elem')
- new_winds: float32 [2, 72, 64, 1024], P(None, None, 'face', 'elem')
The draws below stay inside these ranges and needn't reach their ends.
Inputs may be any that keep to these rules, and one draw needn't show every extreme that they name: depart of element (r, c) is ((r + a) mod 16) * 256 + ((c + b) mod 256) with |a| <= 1 and |b| <= 3; in every device's block of elements both bounds are reached in both directions.
All inputs are finite; a program needn't handle non-finite values.
Results may differ from the reference program's by a relative error of at most 0.0001.
Values sent between devices are 32-bit elements; how exact they have to be, the bound alone decides.
A program may use at most 128 MiB of HBM per device.

```python
import math
import jax
import jax.numpy as jnp
import numpy as np
from jax import lax

LEV = 72
TRAC = 4
EY = 4
EX = 32
SUBSTEPS = 2
RX = 3
RY = 1
OFFS = 64
GY = 16
GX = 256
NY = 64
NX = 1024


def draw_depart(key, part):
    key = jax.random.fold_in(key, 11)
    first, second, third, fourth = jax.random.split(key, 4)
    row_shift = jax.random.randint(first, (GY, GX), -RY, RY + 1)
    col_shift = jax.random.randint(second, (GY, GX), -RX, RX + 1)
    row_flip = jax.random.randint(third, (GY, GX), 0, 2)
    col_flip = jax.random.randint(fourth, (GY, GX), 0, 2)
    row_index = lax.broadcasted_iota(jnp.int32, (GY, GX), 0)
    col_index = lax.broadcasted_iota(jnp.int32, (GY, GX), 1)
    local_row = row_index % EY
    local_col = col_index % EX
    row_shift = jnp.where((local_row == 0) & (row_flip == 1), -RY, row_shift)
    row_shift = jnp.where((local_row == EY - 1) & (row_flip == 1), RY, row_shift)
    col_shift = jnp.where((local_col == 0) & (col_flip == 1), -RX, col_shift)
    col_shift = jnp.where((local_col == EX - 1) & (col_flip == 1), RX, col_shift)
    top_left = (local_row == 0) & (local_col == 0)
    bottom_right = (local_row == EY - 1) & (local_col == EX - 1)
    row_shift = jnp.where(top_left, -RY, jnp.where(bottom_right, RY, row_shift))
    col_shift = jnp.where(top_left, -RX, jnp.where(bottom_right, RX, col_shift))
    source_row = (row_index + row_shift) % GY
    source_col = (col_index + col_shift) % GX
    return (source_row * GX + source_col).astype(jnp.int32)


def touch_ends(values, rng, low, largest):
    longest = values.shape.index(max(values.shape))
    spots = []
    for shift in (0, 1):
        where = [jax.random.randint(jax.random.fold_in(rng, axis), (), 0, length) for axis, length in enumerate(values.shape)]
        where[longest] = (where[longest] + shift) % values.shape[longest]
        spots.append(tuple(where))
    return values.at[spots[0]].set(low).at[spots[1]].set(largest)


def shard_levels(own_key, dims, pieces, low, top_value):
    factor_of, own = 1.0, jax.random.fold_in(own_key, 6)
    for axis_at, parts in pieces:
        heights = jnp.exp(jax.random.uniform(jax.random.fold_in(own, axis_at), (parts,), jnp.float32, low / len(pieces), top_value / len(pieces)))
        factor_of = factor_of * jnp.repeat(heights, dims[axis_at] // parts).reshape([-1 if axis == axis_at else 1 for axis in range(len(dims))])
    return factor_of


def centred(own_key, extent, scale, limit, shards=(), kind=jnp.bfloat16):
    drawn = jax.random.normal(own_key, extent, jnp.float32) * scale
    if len(shards) > 0:
        drawn = shard_levels(own_key, extent, shards, -0.22, 0.18) * drawn
    return jnp.clip(drawn, min=-limit, max=limit).astype(kind)


def setup_inputs(seed: int = 0) -> dict:
    streams_of = jax.random.split(jax.random.key(seed), 7)
    return {
        "tracers": jnp.clip(2.0 * jax.random.uniform(streams_of[0], (TRAC, LEV, NY, NX), jnp.float32) ** shard_levels(streams_of[0], (TRAC, LEV, NY, NX), ((2, 4), (3, 8)), -0.2, 0.2), 0.0, 2.0),
        "thickness": jnp.clip(0.5 + 1.0 * jax.random.uniform(streams_of[1], (LEV, NY, NX), jnp.float32) ** shard_levels(streams_of[1], (LEV, NY, NX), ((1, 4), (2, 8)), -0.2, 0.2), 0.5, 1.5),
        "winds": centred(streams_of[2], (2, LEV, NY, NX), 0.5, 4.0, ((2, 4), (3, 8)), jnp.float32),
        "wave_coef": jnp.clip(jnp.exp(jax.random.uniform(streams_of[3], (LEV,), jnp.float32, math.log(0.02), math.log(0.12))), 0.02, 0.12),
        "depart": draw_depart(jax.random.fold_in(streams_of[6], 71), 0),
        "offsets": touch_ends(jax.random.randint(streams_of[5], (2, NY, NX), 0, OFFS), jax.random.fold_in(streams_of[5], 1), 0, OFFS - 1).astype(jnp.int32),
    }


def gll_points():
    inner = 1.0 / math.sqrt(5.0)
    return [-1.0, -inner, inner, 1.0]

def derivative():
    points = gll_points()
    table = np.zeros((4, 4))
    for target in range(4):
        for source in range(4):
            total_value = 0.0
            for other in range(4):
                if other != source:
                    factor = 1.0 / (points[source] - points[other])
                    for fourth in range(4):
                        if fourth != source and fourth != other:
                            factor = factor * (points[target] - points[fourth]) / (points[source] - points[fourth])
                    total_value = total_value + factor
            table[target, source] = total_value
    return jnp.asarray(table, jnp.float32)

def lagrange(coord):
    points = gll_points()
    values_list = []
    for source in range(4):
        value = jnp.ones_like(coord)
        for other in range(4):
            if other != source:
                value = value * ((coord - points[other]) / (points[source] - points[other]))
        values_list.append(value)
    return jnp.stack(values_list, axis=-1)

def along_columns(field):
    shape = field.shape
    blocks = field.reshape(shape[:-1] + (shape[-1] // 4, 4))
    return jnp.einsum('...m,im->...i', blocks, derivative(), precision=lax.Precision.HIGHEST).reshape(shape)

def along_rows(field):
    shape = field.shape
    blocks = field.reshape(shape[:-2] + (shape[-2] // 4, 4, shape[-1]))
    return jnp.einsum('...mq,im->...iq', blocks, derivative(), precision=lax.Precision.HIGHEST).reshape(shape)

def edge_average(padded):
    inner_cols = padded.shape[-1] - 2
    column_mod = lax.broadcasted_iota(jnp.int32, (inner_cols,), 0) % 4
    middle = padded[..., 1:-1]
    across = jnp.where(column_mod == 3, 0.5 * (middle + padded[..., 2:]), jnp.where(column_mod == 0, 0.5 * (middle + padded[..., :-2]), middle))
    inner_rows = across.shape[-2] - 2
    row_mod = lax.broadcasted_iota(jnp.int32, (inner_rows, 1), 0) % 4
    centre = across[..., 1:-1, :]
    return jnp.where(row_mod == 3, 0.5 * (centre + across[..., 2:, :]), jnp.where(row_mod == 0, 0.5 * (centre + across[..., :-2, :]), centre))

def pad_wrap(field):
    return jnp.pad(field, [(0, 0)] * (field.ndim - 2) + [(1, 1), (1, 1)], mode='wrap')

def wave_substep(height, winds_now, wave_rate, height_pad, wind_pad):
    height = edge_average(height_pad(height - wave_rate * (along_columns(winds_now[0]) + along_rows(winds_now[1]))))
    pushed = jnp.stack([winds_now[0] - wave_rate * along_columns(height), winds_now[1] - wave_rate * along_rows(height)])
    return (height, edge_average(wind_pad(pushed)))

def node_weights(offsets):
    shape = offsets.shape
    blocks = offsets.reshape(2, shape[1] // 4, 4, shape[2] // 4, 4).transpose(0, 1, 3, 2, 4).reshape(2, -1, 16)
    coord = -1.0 + (2.0 * blocks.astype(jnp.float32) + 1.0) / OFFS
    across = lagrange(coord[0])
    upward = lagrange(coord[1])
    return (upward[:, :, :, None] * across[:, :, None, :]).reshape(blocks.shape[1], 16, 16)

def to_grid(values, elem_rows, elem_cols):
    channels = values.shape[0]
    return values.reshape(channels, elem_rows, elem_cols, 4, 4).transpose(0, 1, 3, 2, 4).reshape(channels, 4 * elem_rows, 4 * elem_cols)

def reference(tracers, thickness, winds, wave_coef, depart, offsets):
    wave_rate = wave_coef[:, None, None]
    height = thickness
    winds_now = winds
    for substep in range(SUBSTEPS):
        height, winds_now = wave_substep(height, winds_now, wave_rate, pad_wrap, pad_wrap)
    source_row = (depart // GX).reshape(-1, 1).astype(jnp.int32)
    source_col = (depart % GX).reshape(-1, 1).astype(jnp.int32)
    within = lax.broadcasted_iota(jnp.int32, (16,), 0)
    node_index = ((4 * source_row + within // 4) * NX + 4 * source_col + within % 4).astype(jnp.int32)
    weights = node_weights(offsets)

    def transport(tracer):
        flattened = tracer.reshape(LEV, NY * NX)
        sources = jnp.take(flattened, node_index.reshape(-1), axis=1).reshape(LEV, GY * GX, 16)
        interp = jnp.einsum('cek,ejk->cej', sources, weights, precision=lax.Precision.HIGHEST)
        limited = jnp.clip(interp, lax.optimization_barrier(jnp.min(sources, axis=2, keepdims=True)), lax.optimization_barrier(jnp.max(sources, axis=2, keepdims=True)))
        return to_grid(limited, GY, GX) * height
    tracer_mass = lax.map(transport, tracers)
    return (tracer_mass, height, winds_now)
```

```python
import functools
import math

import jax
import jax.numpy as jnp
import numpy as np
from jax import lax
from jax.experimental import pallas as pl
from jax.experimental.pallas import tpu as pltpu
from jax.sharding import PartitionSpec as P

SUBSTEPS = 2
RX = 3
RY = 1
OFFS = 64


def padded_2(block, sides, width):
    for axis, dim in sides:
        count = lax.axis_size(axis)
        forward = [(i, i + 1) for i in range(count - 1)]
        forward.append((count - 1, 0))
        backward = [(target, source) for source, target in forward]
        low = lax.ppermute(
            lax.slice_in_dim(block, block.shape[dim] - width, None, axis=dim), axis, forward
        )
        high = lax.ppermute(lax.slice_in_dim(block, 0, width, axis=dim), axis, backward)
        block = jnp.concatenate([low, block, high], axis=dim)
    return block


def gll_points():
    inner = 1.0 / math.sqrt(5.0)
    return [-1.0, -inner, inner, 1.0]


def derivative():
    points = gll_points()
    table = np.zeros((4, 4))
    for target in range(4):
        for source in range(4):
            total_value = 0.0
            for other in range(4):
                if other != source:
                    factor = 1.0 / (points[source] - points[other])
                    for fourth in range(4):
                        if fourth != source and fourth != other:
                            factor = (
                                factor
                                * (points[target] - points[fourth])
                                / (points[source] - points[fourth])
                            )
                    total_value = total_value + factor
            table[target, source] = total_value
    return table


def lagrange(coord):
    points = gll_points()
    values_list = []
    for source in range(4):
        value = jnp.ones_like(coord)
        for other in range(4):
            if other != source:
                value = value * ((coord - points[other]) / (points[source] - points[other]))
        values_list.append(value)
    return jnp.stack(values_list, axis=-1)


def along_columns(field):
    count = field.shape[-1] // 4
    matrix = jnp.asarray(np.kron(np.eye(count), derivative().T), jnp.float32)
    return jnp.matmul(field, matrix, precision=lax.Precision.HIGHEST)


def along_rows(field):
    count = field.shape[-2] // 4
    matrix = jnp.asarray(np.kron(np.eye(count), derivative()), jnp.float32)
    return jnp.einsum("ij,...jq->...iq", matrix, field, precision=lax.Precision.HIGHEST)


def edge_average(padded):
    inner_cols = padded.shape[-1] - 2
    column_mod = lax.broadcasted_iota(jnp.int32, (inner_cols,), 0) % 4
    middle = padded[..., 1:-1]
    across = jnp.where(
        column_mod == 3,
        0.5 * (middle + padded[..., 2:]),
        jnp.where(column_mod == 0, 0.5 * (middle + padded[..., :-2]), middle),
    )
    inner_rows = across.shape[-2] - 2
    row_mod = lax.broadcasted_iota(jnp.int32, (inner_rows, 1), 0) % 4
    centre = across[..., 1:-1, :]
    return jnp.where(
        row_mod == 3,
        0.5 * (centre + across[..., 2:, :]),
        jnp.where(row_mod == 0, 0.5 * (centre + across[..., :-2, :]), centre),
    )


def height_rim(field):
    return padded_2(field, (("face", 1), ("elem", 2)), 1)


def wind_rim(field):
    return padded_2(field, (("face", 2), ("elem", 3)), 1)


def wave_substep(height, winds_now, wave_rate, height_pad, wind_pad):
    height = edge_average(
        height_pad(height - wave_rate * (along_columns(winds_now[0]) + along_rows(winds_now[1])))
    )
    pushed = jnp.stack(
        [
            winds_now[0] - wave_rate * along_columns(height),
            winds_now[1] - wave_rate * along_rows(height),
        ]
    )
    return (height, edge_average(wind_pad(pushed)))


def node_weights(offsets):
    coord = -1.0 + (2.0 * offsets.astype(jnp.float32) + 1.0) / OFFS
    across = lagrange(coord[0])
    upward = lagrange(coord[1])
    weights = upward[..., :, None] * across[..., None, :]
    return weights.reshape(offsets.shape[1], offsets.shape[2], 16).transpose(2, 0, 1)


def shift_both(forward_piece, backward_piece, axis):
    count = lax.axis_size(axis)
    forward = [(i, (i + 1) % count) for i in range(count)]
    backward = [(target, source) for source, target in forward]
    return lax.ppermute(forward_piece, axis, forward), lax.ppermute(backward_piece, axis, backward)


def transport_kernel(elem_rows, levels, low, main, high, halo, target, weights, height, out, parts, picked):
    channels = main.shape[1]
    cols = main.shape[2]
    for row in range(4 * (elem_rows + 2)):
        if row < 4:
            middle = low[row]
        elif row < 4 * (elem_rows + 1):
            middle = main[row - 4]
        else:
            middle = high[row - 4 * (elem_rows + 1)]
        whole = jnp.concatenate([middle, halo[row]], axis=1)
        coarse = whole.astype(jnp.bfloat16)
        fine = (whole - coarse.astype(jnp.float32)).astype(jnp.bfloat16)
        at = pl.ds((row % 4) * channels, channels)
        parts[row // 4, 0, at, :] = coarse
        parts[row // 4, 1, at, :] = fine
    width = parts.shape[-1]
    chunk = 24
    for er in range(elem_rows):
        place = lax.broadcasted_iota(jnp.int32, (3 * width, 4 * cols), 0)
        hot = jnp.where(place == target[er : er + 1, :], 1.0, 0.0).astype(jnp.bfloat16)
        for m in range(4):
            at = pl.ds(m * channels, channels)
            total = None
            for piece in range(2):
                left = jnp.concatenate([parts[er + k, piece, at, :] for k in range(3)], axis=1)
                term = jnp.dot(left, hot, preferred_element_type=jnp.float32)
                total = term if total is None else total + term
            picked[m] = total

        @pl.loop(0, channels // chunk)
        def _(step, er=er):
            start = pl.multiple_of(step * chunk, 8)
            level = pl.multiple_of(lax.rem(step, levels // chunk) * chunk, 8)
            nodes = [
                picked[m, pl.ds(start, chunk), n * cols : (n + 1) * cols]
                for m in range(4)
                for n in range(4)
            ]
            lowest = nodes[0]
            highest = nodes[0]
            for node in nodes[1:]:
                lowest = jnp.minimum(lowest, node)
                highest = jnp.maximum(highest, node)
            for a in range(4):
                row = 4 * er + a
                value = weights[0, row : row + 1, :] * nodes[0]
                for s in range(1, 16):
                    value = value + weights[s, row : row + 1, :] * nodes[s]
                value = jnp.minimum(jnp.maximum(value, lowest), highest)
                out[pl.ds(start, chunk), row, :] = value * height[row, pl.ds(level, chunk), :]


def transport(tracers, height, depart, offsets):
    count, levels, node_rows, node_cols = tracers.shape
    elem_rows = node_rows // 4
    elem_cols = node_cols // 4
    channels = count * levels
    face_at = lax.axis_index("face")
    elem_at = lax.axis_index("elem")
    grid_rows = elem_rows * lax.axis_size("face")
    grid_cols = elem_cols * lax.axis_size("elem")
    rows_first = tracers.reshape(channels, node_rows, node_cols).transpose(1, 0, 2)
    low, high = shift_both(rows_first[-4:], rows_first[:4], "face")
    edge = 4 * RX
    left, right = shift_both(
        rows_first[:, :, -edge:].transpose(0, 2, 1), rows_first[:, :, :edge].transpose(0, 2, 1), "elem"
    )
    sides = jnp.concatenate([left, right], axis=1)
    under, above = shift_both(sides[-4:], sides[:4], "face")
    sides = jnp.concatenate([under, sides, above], axis=0)
    halo = jnp.pad(sides, ((0, 0), (0, node_cols - 2 * edge), (0, 0))).transpose(0, 2, 1)

    row_index = lax.broadcasted_iota(jnp.int32, (elem_rows, elem_cols), 0)
    col_index = lax.broadcasted_iota(jnp.int32, (elem_rows, elem_cols), 1)
    source_row = depart // grid_cols
    source_col = depart % grid_cols
    row_shift = (source_row - (face_at * elem_rows + row_index) + RY) % grid_rows
    col_shift = (source_col - (elem_at * elem_cols + col_index) + RX) % grid_cols - RX
    first = jnp.repeat(4 * (col_index + col_shift), 4, axis=1)
    which = jnp.repeat(row_shift, 4, axis=1)
    width = 2 * node_cols
    targets = []
    for n in range(4):
        col = first + n
        spot = jnp.where(col < 0, node_cols + edge + col, jnp.where(col < node_cols, col, col + edge))
        targets.append(which * width + spot)
    target = jnp.concatenate(targets, axis=1)
    weights = node_weights(offsets)
    out = pl.pallas_call(
        functools.partial(transport_kernel, elem_rows, levels),
        out_shape=jax.ShapeDtypeStruct((channels, node_rows, node_cols), jnp.float32),
        in_specs=[pl.BlockSpec(memory_space=pltpu.VMEM)] * 7,
        out_specs=pl.BlockSpec(memory_space=pltpu.VMEM),
        scratch_shapes=[
            pltpu.VMEM((elem_rows + 2, 2, 4 * channels, width), jnp.bfloat16),
            pltpu.VMEM((4, channels, 4 * node_cols), jnp.float32),
        ],
        compiler_params=pltpu.CompilerParams(vmem_limit_bytes=48 * 1024 * 1024),
        name="transport",
    )(low, rows_first, high, halo, target, weights, height.transpose(1, 0, 2))
    return out.reshape(tracers.shape)


def body(tracers, thickness, winds, wave_coef, depart, offsets):
    wave_rate = wave_coef[:, None, None]
    height = thickness
    winds_now = winds
    for substep in range(SUBSTEPS):
        height, winds_now = wave_substep(height, winds_now, wave_rate, height_rim, wind_rim)
    return (transport(tracers, height, depart, offsets), height, winds_now)


def solution(mesh):
    in_specs = (
        P(None, None, "face", "elem"),
        P(None, "face", "elem"),
        P(None, None, "face", "elem"),
        P(),
        P("face", "elem"),
        P(None, "face", "elem"),
    )
    out_specs = (
        P(None, None, "face", "elem"),
        P(None, "face", "elem"),
        P(None, None, "face", "elem"),
    )
    return jax.shard_map(body, mesh=mesh, in_specs=in_specs, out_specs=out_specs, check_vma=False)
```

```python
import functools
import math

import jax
import jax.numpy as jnp
import numpy as np
from jax import lax
from jax.experimental import pallas as pl
from jax.experimental.pallas import tpu as pltpu
from jax.sharding import PartitionSpec as P

SUBSTEPS = 2
RX = 3
RY = 1
OFFS = 64


def gll_points():
    inner = 1.0 / math.sqrt(5.0)
    return [-1.0, -inner, inner, 1.0]


def derivative():
    points = gll_points()
    table = np.zeros((4, 4))
    for target in range(4):
        for source in range(4):
            total_value = 0.0
            for other in range(4):
                if other != source:
                    factor = 1.0 / (points[source] - points[other])
                    for fourth in range(4):
                        if fourth != source and fourth != other:
                            factor = (
                                factor
                                * (points[target] - points[fourth])
                                / (points[source] - points[fourth])
                            )
                    total_value = total_value + factor
            table[target, source] = total_value
    return table


def lagrange(coord):
    points = gll_points()
    values_list = []
    for source in range(4):
        value = jnp.ones_like(coord)
        for other in range(4):
            if other != source:
                value = value * ((coord - points[other]) / (points[source] - points[other]))
        values_list.append(value)
    return jnp.stack(values_list, axis=-1)


def roll_table():
    table = derivative()
    shifts = np.zeros((7, 4))
    for target in range(4):
        for source in range(4):
            shifts[source - target + 3, target] = table[target, source]
    return shifts


def apply_shifts(field, table, axis):
    size = field.shape[axis]
    total = field * table[3][None]
    for k in (-3, -2, -1, 1, 2, 3):
        total = total + pltpu.roll(field, (-k) % size, axis) * table[k + 3][None]
    return total


def wave_kernel(
    thickness, winds, rate, by_col, by_row, take, put, height, winds_out,
    fresh, across, side, col_send, col_recv, row_send, row_recv, send_sem, recv_sem,
):
    levels, rows, cols = thickness.shape
    chunk = 8
    neighbours = []
    for axis in ("elem", "face"):
        count = lax.axis_size(axis)
        here = lax.axis_index(axis)
        neighbours.append((axis, lax.rem(here + 1, count), lax.rem(here + count - 1, count)))
    barrier = pltpu.get_barrier_semaphore()
    for axis, up, down in neighbours:
        for place in (up, down):
            pl.semaphore_signal(
                barrier, inc=1, device_id={axis: place}, device_id_type=pl.DeviceIdType.MESH
            )
    pl.semaphore_wait(barrier, 4)

    lane = lax.broadcasted_iota(jnp.int32, (rows, cols), 1)
    line = lax.broadcasted_iota(jnp.int32, (rows, cols), 0)

    def masks(position, size):
        later = jnp.where((position % 4 == 3) & (position != size - 1), 0.5, 0.0)
        earlier = jnp.where((position % 4 == 0) & (position != 0), 0.5, 0.0)
        own = jnp.where((position % 4 == 0) | (position % 4 == 3), 0.5, 1.0)
        return own[None], later[None], earlier[None]

    def exchange(number, which, sources, targets):
        axis, up, down = neighbours[which]
        copies = []
        for way, place in ((0, up), (1, down)):
            copies.append(
                pltpu.make_async_remote_copy(
                    src_ref=sources[way],
                    dst_ref=targets[way],
                    send_sem=send_sem.at[number, which, way],
                    recv_sem=recv_sem.at[number, which, way],
                    device_id={axis: place},
                    device_id_type=pl.DeviceIdType.MESH,
                )
            )
        for copy in copies:
            copy.start()
        for copy in copies:
            copy.wait()

    def average(number, count, store):
        edges = None
        for f in range(count):
            flat = fresh[f].reshape(levels * rows, cols)
            term = lax.dot_general(
                take[f], flat, (((1,), (1,)), ((), ())),
                precision=lax.Precision.HIGHEST, preferred_element_type=jnp.float32,
            )
            edges = term if edges is None else edges + term
        col_send[number] = edges
        exchange(
            number, 0,
            (col_send.at[number], col_send.at[number]),
            (col_recv.at[number, 0], col_recv.at[number, 1]),
        )
        both = jnp.concatenate([col_recv[number, 0], col_recv[number, 1]], axis=0)
        own, later, earlier = masks(lane, cols)
        for f in range(count):
            spread = lax.dot_general(
                both, put[f], (((0,), (0,)), ((), ())),
                precision=lax.Precision.HIGHEST, preferred_element_type=jnp.float32,
            )
            side[f] = spread.reshape(levels, rows, cols)

            @pl.loop(0, levels // chunk)
            def _(step, f=f):
                at = pl.ds(pl.multiple_of(step * chunk, chunk), chunk)
                field = fresh[f, at]
                mixed = field * own + pltpu.roll(field, cols - 1, 2) * later
                mixed = mixed + pltpu.roll(field, 1, 2) * earlier + side[f, at]
                across[f, at] = mixed
                row_send[number, 0, f, at, :] = mixed[:, rows - 1, :]
                row_send[number, 1, f, at, :] = mixed[:, 0, :]

        exchange(
            number, 1,
            (row_send.at[number, 0, pl.ds(0, count)], row_send.at[number, 1, pl.ds(0, count)]),
            (row_recv.at[number, 0, pl.ds(0, count)], row_recv.at[number, 1, pl.ds(0, count)]),
        )
        own_row, later_row, earlier_row = masks(line, rows)
        first = jnp.where(line == 0, 0.5, 0.0)[None]
        last = jnp.where(line == rows - 1, 0.5, 0.0)[None]
        for f in range(count):

            @pl.loop(0, levels // chunk)
            def _(step, f=f):
                at = pl.ds(pl.multiple_of(step * chunk, chunk), chunk)
                field = across[f, at]
                mixed = field * own_row + pltpu.roll(field, rows - 1, 1) * later_row
                mixed = mixed + pltpu.roll(field, 1, 1) * earlier_row
                mixed = mixed + first * row_recv[number, 0, f, at, :][:, None, :]
                mixed = mixed + last * row_recv[number, 1, f, at, :][:, None, :]
                store(f, at, mixed)

    def store_height(f, at, value):
        height[at] = value

    def store_winds(f, at, value):
        winds_out[f, at] = value

    for substep in range(SUBSTEPS):
        old_height = thickness if substep == 0 else height
        old_winds = winds if substep == 0 else winds_out

        @pl.loop(0, levels // chunk)
        def _(step):
            at = pl.ds(pl.multiple_of(step * chunk, chunk), chunk)
            flow = apply_shifts(old_winds[0, at], by_col, 2) + apply_shifts(old_winds[1, at], by_row, 1)
            fresh[0, at] = old_height[at] - rate[at] * flow

        average(2 * substep, 1, store_height)

        @pl.loop(0, levels // chunk)
        def _(step):
            at = pl.ds(pl.multiple_of(step * chunk, chunk), chunk)
            now = height[at]
            fresh[0, at] = old_winds[0, at] - rate[at] * apply_shifts(now, by_col, 2)
            fresh[1, at] = old_winds[1, at] - rate[at] * apply_shifts(now, by_row, 1)

        average(2 * substep + 1, 2, store_winds)


def waves(thickness, winds, wave_coef):
    levels, rows, cols = thickness.shape
    shifts = roll_table()
    by_col = jnp.asarray(np.broadcast_to(np.tile(shifts, (1, cols // 4))[:, None, :], (7, rows, cols)), jnp.float32)
    by_row = jnp.asarray(np.broadcast_to(np.tile(shifts, (1, rows // 4))[:, :, None], (7, rows, cols)), jnp.float32)
    take = np.zeros((2, 8, cols))
    put = np.zeros((2, 16, cols))
    for f in range(2):
        take[f, 2 * f, 0] = 1.0
        take[f, 2 * f + 1, cols - 1] = 1.0
        put[f, 2 * f + 1, 0] = 0.5
        put[f, 8 + 2 * f, cols - 1] = 0.5
    rate = jnp.broadcast_to(wave_coef[:, None, None], (levels, 1, cols))
    rounds = 2 * SUBSTEPS
    wide = levels * rows
    return pl.pallas_call(
        wave_kernel,
        out_shape=(
            jax.ShapeDtypeStruct(thickness.shape, jnp.float32),
            jax.ShapeDtypeStruct(winds.shape, jnp.float32),
        ),
        in_specs=[pl.BlockSpec(memory_space=pltpu.VMEM)] * 7,
        out_specs=(pl.BlockSpec(memory_space=pltpu.VMEM), pl.BlockSpec(memory_space=pltpu.VMEM)),
        scratch_shapes=[
            pltpu.VMEM(winds.shape, jnp.float32),
            pltpu.VMEM(winds.shape, jnp.float32),
            pltpu.VMEM(winds.shape, jnp.float32),
            pltpu.VMEM((rounds, 8, wide), jnp.float32),
            pltpu.VMEM((rounds, 2, 8, wide), jnp.float32),
            pltpu.VMEM((rounds, 2, 2, levels, cols), jnp.float32),
            pltpu.VMEM((rounds, 2, 2, levels, cols), jnp.float32),
            pltpu.SemaphoreType.DMA((rounds, 2, 2)),
            pltpu.SemaphoreType.DMA((rounds, 2, 2)),
        ],
        compiler_params=pltpu.CompilerParams(
            collective_id=0, has_side_effects=True, vmem_limit_bytes=40 * 1024 * 1024
        ),
        cost_estimate=pl.CostEstimate(flops=300000000, bytes_accessed=60000000, transcendentals=0),
        name="waves",
    )(
        thickness, winds, rate, by_col, by_row,
        jnp.asarray(take, jnp.float32), jnp.asarray(put, jnp.float32),
    )


def node_weights(offsets):
    coord = -1.0 + (2.0 * offsets.astype(jnp.float32) + 1.0) / OFFS
    across = lagrange(coord[0])
    upward = lagrange(coord[1])
    weights = upward[..., :, None] * across[..., None, :]
    return weights.reshape(offsets.shape[1], offsets.shape[2], 16).transpose(2, 0, 1)


def shift_both(forward_piece, backward_piece, axis):
    count = lax.axis_size(axis)
    forward = [(i, (i + 1) % count) for i in range(count)]
    backward = [(target, source) for source, target in forward]
    return lax.ppermute(forward_piece, axis, forward), lax.ppermute(backward_piece, axis, backward)


def transport_kernel(elem_rows, levels, low, main, high, halo, target, weights, height, out, parts, picked):
    channels = main.shape[1]
    cols = main.shape[2]
    for row in range(4 * (elem_rows + 2)):
        if row < 4:
            middle = low[row]
        elif row < 4 * (elem_rows + 1):
            middle = main[row - 4]
        else:
            middle = high[row - 4 * (elem_rows + 1)]
        whole = jnp.concatenate([middle, halo[row]], axis=1)
        coarse = whole.astype(jnp.bfloat16)
        fine = (whole - coarse.astype(jnp.float32)).astype(jnp.bfloat16)
        at = pl.ds((row % 4) * channels, channels)
        parts[row // 4, 0, at, :] = coarse
        parts[row // 4, 1, at, :] = fine
    width = parts.shape[-1]
    chunk = 24
    for er in range(elem_rows):
        place = lax.broadcasted_iota(jnp.int32, (3 * width, 4 * cols), 0)
        hot = jnp.where(place == target[er : er + 1, :], 1.0, 0.0).astype(jnp.bfloat16)
        for m in range(4):
            at = pl.ds(m * channels, channels)
            total = None
            for piece in range(2):
                left = jnp.concatenate([parts[er + k, piece, at, :] for k in range(3)], axis=1)
                term = jnp.dot(left, hot, preferred_element_type=jnp.float32)
                total = term if total is None else total + term
            picked[m] = total

        @pl.loop(0, channels // chunk)
        def _(step, er=er):
            start = pl.multiple_of(step * chunk, 8)
            level = pl.multiple_of(lax.rem(step, levels // chunk) * chunk, 8)
            nodes = [
                picked[m, pl.ds(start, chunk), n * cols : (n + 1) * cols]
                for m in range(4)
                for n in range(4)
            ]
            lowest = nodes[0]
            highest = nodes[0]
            for node in nodes[1:]:
                lowest = jnp.minimum(lowest, node)
                highest = jnp.maximum(highest, node)
            for a in range(4):
                row = 4 * er + a
                value = weights[0, row : row + 1, :] * nodes[0]
                for s in range(1, 16):
                    value = value + weights[s, row : row + 1, :] * nodes[s]
                value = jnp.minimum(jnp.maximum(value, lowest), highest)
                out[pl.ds(start, chunk), row, :] = value * height[row, pl.ds(level, chunk), :]


def transport(tracers, height, depart, offsets):
    count, levels, node_rows, node_cols = tracers.shape
    elem_rows = node_rows // 4
    elem_cols = node_cols // 4
    channels = count * levels
    face_at = lax.axis_index("face")
    elem_at = lax.axis_index("elem")
    grid_rows = elem_rows * lax.axis_size("face")
    grid_cols = elem_cols * lax.axis_size("elem")
    rows_first = tracers.reshape(channels, node_rows, node_cols).transpose(1, 0, 2)
    low, high = shift_both(rows_first[-4:], rows_first[:4], "face")
    edge = 4 * RX
    left, right = shift_both(
        rows_first[:, :, -edge:].transpose(0, 2, 1), rows_first[:, :, :edge].transpose(0, 2, 1), "elem"
    )
    sides = jnp.concatenate([left, right], axis=1)
    under, above = shift_both(sides[-4:], sides[:4], "face")
    sides = jnp.concatenate([under, sides, above], axis=0)
    halo = jnp.pad(sides, ((0, 0), (0, node_cols - 2 * edge), (0, 0))).transpose(0, 2, 1)

    row_index = lax.broadcasted_iota(jnp.int32, (elem_rows, elem_cols), 0)
    col_index = lax.broadcasted_iota(jnp.int32, (elem_rows, elem_cols), 1)
    source_row = depart // grid_cols
    source_col = depart % grid_cols
    row_shift = (source_row - (face_at * elem_rows + row_index) + RY) % grid_rows
    col_shift = (source_col - (elem_at * elem_cols + col_index) + RX) % grid_cols - RX
    first = jnp.repeat(4 * (col_index + col_shift), 4, axis=1)
    which = jnp.repeat(row_shift, 4, axis=1)
    width = 2 * node_cols
    targets = []
    for n in range(4):
        col = first + n
        spot = jnp.where(col < 0, node_cols + edge + col, jnp.where(col < node_cols, col, col + edge))
        targets.append(which * width + spot)
    target = jnp.concatenate(targets, axis=1)
    weights = node_weights(offsets)
    out = pl.pallas_call(
        functools.partial(transport_kernel, elem_rows, levels),
        out_shape=jax.ShapeDtypeStruct((channels, node_rows, node_cols), jnp.float32),
        in_specs=[pl.BlockSpec(memory_space=pltpu.VMEM)] * 7,
        out_specs=pl.BlockSpec(memory_space=pltpu.VMEM),
        scratch_shapes=[
            pltpu.VMEM((elem_rows + 2, 2, 4 * channels, width), jnp.bfloat16),
            pltpu.VMEM((4, channels, 4 * node_cols), jnp.float32),
        ],
        compiler_params=pltpu.CompilerParams(vmem_limit_bytes=48 * 1024 * 1024),
        name="transport",
    )(low, rows_first, high, halo, target, weights, height.transpose(1, 0, 2))
    return out.reshape(tracers.shape)


def body(tracers, thickness, winds, wave_coef, depart, offsets):
    height, winds_now = waves(thickness, winds, wave_coef)
    return (transport(tracers, height, depart, offsets), height, winds_now)


def solution(mesh):
    in_specs = (
        P(None, None, "face", "elem"),
        P(None, "face", "elem"),
        P(None, None, "face", "elem"),
        P(),
        P("face", "elem"),
        P(None, "face", "elem"),
    )
    out_specs = (
        P(None, None, "face", "elem"),
        P(None, "face", "elem"),
        P(None, None, "face", "elem"),
    )
    return jax.shard_map(body, mesh=mesh, in_specs=in_specs, out_specs=out_specs, check_vma=False)
```

```python
import functools
import math

import jax
import jax.numpy as jnp
import numpy as np
from jax import lax
from jax.experimental import pallas as pl
from jax.experimental.pallas import tpu as pltpu
from jax.sharding import PartitionSpec as P

SUBSTEPS = 2
RX = 3
RY = 1
OFFS = 64


def gll_points():
    inner = 1.0 / math.sqrt(5.0)
    return [-1.0, -inner, inner, 1.0]


def derivative():
    points = gll_points()
    table = np.zeros((4, 4))
    for target in range(4):
        for source in range(4):
            total_value = 0.0
            for other in range(4):
                if other != source:
                    factor = 1.0 / (points[source] - points[other])
                    for fourth in range(4):
                        if fourth != source and fourth != other:
                            factor = (
                                factor
                                * (points[target] - points[fourth])
                                / (points[source] - points[fourth])
                            )
                    total_value = total_value + factor
            table[target, source] = total_value
    return table


def lagrange(coord):
    points = gll_points()
    values_list = []
    for source in range(4):
        value = jnp.ones_like(coord)
        for other in range(4):
            if other != source:
                value = value * ((coord - points[other]) / (points[source] - points[other]))
        values_list.append(value)
    return jnp.stack(values_list, axis=-1)


def roll_table():
    table = derivative()
    shifts = np.zeros((7, 4))
    for target in range(4):
        for source in range(4):
            shifts[source - target + 3, target] = table[target, source]
    return shifts


def apply_shifts(field, table, axis):
    size = field.shape[axis]
    total = field * table[3][None]
    for k in (-3, -2, -1, 1, 2, 3):
        total = total + pltpu.roll(field, (-k) % size, axis) * table[k + 3][None]
    return total


def selected(table, values, dim, values_first):
    table = table.astype(jnp.bfloat16)
    total = None
    rest = values
    for _ in range(3):
        piece = rest.astype(jnp.bfloat16)
        rest = rest - piece.astype(jnp.float32)
        pair = (piece, table) if values_first else (table, piece)
        term = lax.dot_general(
            *pair, (((dim,), (dim,)), ((), ())), preferred_element_type=jnp.float32
        )
        total = term if total is None else total + term
    return total


def wave_kernel(
    thickness, winds, rate, by_col, by_row, take, put, height, winds_out,
    fresh, across, side, col_send, col_recv, row_send, row_recv, send_sem, recv_sem,
):
    levels, rows, cols = thickness.shape
    chunk = 8
    neighbours = []
    for axis in ("elem", "face"):
        count = lax.axis_size(axis)
        here = lax.axis_index(axis)
        neighbours.append((axis, lax.rem(here + 1, count), lax.rem(here + count - 1, count)))
    barrier = pltpu.get_barrier_semaphore()
    for axis, up, down in neighbours:
        for place in (up, down):
            pl.semaphore_signal(
                barrier, inc=1, device_id={axis: place}, device_id_type=pl.DeviceIdType.MESH
            )
    pl.semaphore_wait(barrier, 4)

    lane = lax.broadcasted_iota(jnp.int32, (rows, cols), 1)
    line = lax.broadcasted_iota(jnp.int32, (rows, cols), 0)

    def masks(position, size):
        later = jnp.where((position % 4 == 3) & (position != size - 1), 0.5, 0.0)
        earlier = jnp.where((position % 4 == 0) & (position != 0), 0.5, 0.0)
        own = jnp.where((position % 4 == 0) | (position % 4 == 3), 0.5, 1.0)
        return own[None], later[None], earlier[None]

    def exchange(number, which, sources, targets):
        axis, up, down = neighbours[which]
        copies = []
        for way, place in ((0, up), (1, down)):
            copies.append(
                pltpu.make_async_remote_copy(
                    src_ref=sources[way],
                    dst_ref=targets[way],
                    send_sem=send_sem.at[number, which, way],
                    recv_sem=recv_sem.at[number, which, way],
                    device_id={axis: place},
                    device_id_type=pl.DeviceIdType.MESH,
                )
            )
        for copy in copies:
            copy.start()
        for copy in copies:
            copy.wait()

    def average(number, count, store):
        edges = None
        for f in range(count):
            flat = fresh[f].reshape(levels * rows, cols)
            term = selected(take[f], flat, 1, False)
            edges = term if edges is None else edges + term
        col_send[number] = edges
        exchange(
            number, 0,
            (col_send.at[number], col_send.at[number]),
            (col_recv.at[number, 0], col_recv.at[number, 1]),
        )
        both = jnp.concatenate([col_recv[number, 0], col_recv[number, 1]], axis=0)
        own, later, earlier = masks(lane, cols)
        for f in range(count):
            spread = selected(put[f], both, 0, True)
            side[f] = spread.reshape(levels, rows, cols)

            @pl.loop(0, levels // chunk)
            def _(step, f=f):
                at = pl.ds(pl.multiple_of(step * chunk, chunk), chunk)
                field = fresh[f, at]
                mixed = field * own + pltpu.roll(field, cols - 1, 2) * later
                mixed = mixed + pltpu.roll(field, 1, 2) * earlier + side[f, at]
                across[f, at] = mixed
                row_send[number, 0, f, at, :] = mixed[:, rows - 1, :]
                row_send[number, 1, f, at, :] = mixed[:, 0, :]

        exchange(
            number, 1,
            (row_send.at[number, 0, pl.ds(0, count)], row_send.at[number, 1, pl.ds(0, count)]),
            (row_recv.at[number, 0, pl.ds(0, count)], row_recv.at[number, 1, pl.ds(0, count)]),
        )
        own_row, later_row, earlier_row = masks(line, rows)
        first = jnp.where(line == 0, 0.5, 0.0)[None]
        last = jnp.where(line == rows - 1, 0.5, 0.0)[None]
        for f in range(count):

            @pl.loop(0, levels // chunk)
            def _(step, f=f):
                at = pl.ds(pl.multiple_of(step * chunk, chunk), chunk)
                field = across[f, at]
                mixed = field * own_row + pltpu.roll(field, rows - 1, 1) * later_row
                mixed = mixed + pltpu.roll(field, 1, 1) * earlier_row
                mixed = mixed + first * row_recv[number, 0, f, at, :][:, None, :]
                mixed = mixed + last * row_recv[number, 1, f, at, :][:, None, :]
                store(f, at, mixed)

    def store_height(f, at, value):
        height[at] = value

    def store_winds(f, at, value):
        winds_out[f, at] = value

    for substep in range(SUBSTEPS):
        old_height = thickness if substep == 0 else height
        old_winds = winds if substep == 0 else winds_out

        @pl.loop(0, levels // chunk)
        def _(step):
            at = pl.ds(pl.multiple_of(step * chunk, chunk), chunk)
            flow = apply_shifts(old_winds[0, at], by_col, 2) + apply_shifts(old_winds[1, at], by_row, 1)
            fresh[0, at] = old_height[at] - rate[at] * flow

        average(2 * substep, 1, store_height)

        @pl.loop(0, levels // chunk)
        def _(step):
            at = pl.ds(pl.multiple_of(step * chunk, chunk), chunk)
            now = height[at]
            fresh[0, at] = old_winds[0, at] - rate[at] * apply_shifts(now, by_col, 2)
            fresh[1, at] = old_winds[1, at] - rate[at] * apply_shifts(now, by_row, 1)

        average(2 * substep + 1, 2, store_winds)


def waves(thickness, winds, wave_coef):
    levels, rows, cols = thickness.shape
    shifts = roll_table()
    by_col = jnp.asarray(np.broadcast_to(np.tile(shifts, (1, cols // 4))[:, None, :], (7, rows, cols)), jnp.float32)
    by_row = jnp.asarray(np.broadcast_to(np.tile(shifts, (1, rows // 4))[:, :, None], (7, rows, cols)), jnp.float32)
    take = np.zeros((2, 8, cols))
    put = np.zeros((2, 16, cols))
    for f in range(2):
        take[f, 2 * f, 0] = 1.0
        take[f, 2 * f + 1, cols - 1] = 1.0
        put[f, 2 * f + 1, 0] = 0.5
        put[f, 8 + 2 * f, cols - 1] = 0.5
    rate = jnp.broadcast_to(wave_coef[:, None, None], (levels, 1, cols))
    rounds = 2 * SUBSTEPS
    wide = levels * rows
    return pl.pallas_call(
        wave_kernel,
        out_shape=(
            jax.ShapeDtypeStruct(thickness.shape, jnp.float32),
            jax.ShapeDtypeStruct(winds.shape, jnp.float32),
        ),
        in_specs=[pl.BlockSpec(memory_space=pltpu.VMEM)] * 7,
        out_specs=(pl.BlockSpec(memory_space=pltpu.VMEM), pl.BlockSpec(memory_space=pltpu.VMEM)),
        scratch_shapes=[
            pltpu.VMEM(winds.shape, jnp.float32),
            pltpu.VMEM(winds.shape, jnp.float32),
            pltpu.VMEM(winds.shape, jnp.float32),
            pltpu.VMEM((rounds, 8, wide), jnp.float32),
            pltpu.VMEM((rounds, 2, 8, wide), jnp.float32),
            pltpu.VMEM((rounds, 2, 2, levels, cols), jnp.float32),
            pltpu.VMEM((rounds, 2, 2, levels, cols), jnp.float32),
            pltpu.SemaphoreType.DMA((rounds, 2, 2)),
            pltpu.SemaphoreType.DMA((rounds, 2, 2)),
        ],
        compiler_params=pltpu.CompilerParams(
            collective_id=0, has_side_effects=True, vmem_limit_bytes=40 * 1024 * 1024
        ),
        cost_estimate=pl.CostEstimate(flops=300000000, bytes_accessed=60000000, transcendentals=0),
        name="waves",
    )(
        thickness, winds, rate, by_col, by_row,
        jnp.asarray(take, jnp.float32), jnp.asarray(put, jnp.float32),
    )


def node_weights(offsets):
    coord = -1.0 + (2.0 * offsets.astype(jnp.float32) + 1.0) / OFFS
    across = lagrange(coord[0])
    upward = lagrange(coord[1])
    weights = upward[..., :, None] * across[..., None, :]
    return weights.reshape(offsets.shape[1], offsets.shape[2], 16).transpose(2, 0, 1)


def shift_both(forward_piece, backward_piece, axis):
    count = lax.axis_size(axis)
    forward = [(i, (i + 1) % count) for i in range(count)]
    backward = [(target, source) for source, target in forward]
    return lax.ppermute(forward_piece, axis, forward), lax.ppermute(backward_piece, axis, backward)


def transport_kernel(elem_rows, levels, low, main, high, halo, target, weights, height, out, parts, picked):
    channels = main.shape[1]
    cols = main.shape[2]
    for row in range(4 * (elem_rows + 2)):
        if row < 4:
            middle = low[row]
        elif row < 4 * (elem_rows + 1):
            middle = main[row - 4]
        else:
            middle = high[row - 4 * (elem_rows + 1)]
        whole = jnp.concatenate([middle, halo[row]], axis=1)
        coarse = whole.astype(jnp.bfloat16)
        fine = (whole - coarse.astype(jnp.float32)).astype(jnp.bfloat16)
        at = pl.ds((row % 4) * channels, channels)
        parts[row // 4, 0, at, :] = coarse
        parts[row // 4, 1, at, :] = fine
    width = parts.shape[-1]
    chunk = 24
    for er in range(elem_rows):
        place = lax.broadcasted_iota(jnp.int32, (3 * width, 4 * cols), 0)
        hot = jnp.where(place == target[er : er + 1, :], 1.0, 0.0).astype(jnp.bfloat16)
        for m in range(4):
            at = pl.ds(m * channels, channels)
            total = None
            for piece in range(2):
                left = jnp.concatenate([parts[er + k, piece, at, :] for k in range(3)], axis=1)
                term = jnp.dot(left, hot, preferred_element_type=jnp.float32)
                total = term if total is None else total + term
            picked[m] = total

        @pl.loop(0, channels // chunk)
        def _(step, er=er):
            start = pl.multiple_of(step * chunk, 8)
            level = pl.multiple_of(lax.rem(step, levels // chunk) * chunk, 8)
            nodes = [
                picked[m, pl.ds(start, chunk), n * cols : (n + 1) * cols]
                for m in range(4)
                for n in range(4)
            ]
            lowest = nodes[0]
            highest = nodes[0]
            for node in nodes[1:]:
                lowest = jnp.minimum(lowest, node)
                highest = jnp.maximum(highest, node)
            for a in range(4):
                row = 4 * er + a
                value = weights[0, row : row + 1, :] * nodes[0]
                for s in range(1, 16):
                    value = value + weights[s, row : row + 1, :] * nodes[s]
                value = jnp.minimum(jnp.maximum(value, lowest), highest)
                out[pl.ds(start, chunk), row, :] = value * height[row, pl.ds(level, chunk), :]


def step(tracers, thickness, winds, wave_coef, depart, offsets):
    count, levels, node_rows, node_cols = tracers.shape
    elem_rows = node_rows // 4
    elem_cols = node_cols // 4
    channels = count * levels
    face_at = lax.axis_index("face")
    elem_at = lax.axis_index("elem")
    grid_rows = elem_rows * lax.axis_size("face")
    grid_cols = elem_cols * lax.axis_size("elem")
    rows_first = tracers.reshape(channels, node_rows, node_cols).transpose(1, 0, 2)
    edge = 4 * RX
    left, right = shift_both(
        rows_first[:, :, -edge:].transpose(0, 2, 1), rows_first[:, :, :edge].transpose(0, 2, 1), "elem"
    )
    sides = jnp.concatenate([left, right], axis=1)
    under, above = shift_both(sides[-4:], sides[:4], "face")
    sides = jnp.concatenate([under, sides, above], axis=0)
    halo = jnp.pad(sides, ((0, 0), (0, node_cols - 2 * edge), (0, 0))).transpose(0, 2, 1)
    halo, rows_first, thickness, winds = lax.optimization_barrier((halo, rows_first, thickness, winds))
    low, high = shift_both(rows_first[-4:], rows_first[:4], "face")
    height, new_winds = waves(thickness, winds, wave_coef)

    row_index = lax.broadcasted_iota(jnp.int32, (elem_rows, elem_cols), 0)
    col_index = lax.broadcasted_iota(jnp.int32, (elem_rows, elem_cols), 1)
    source_row = depart // grid_cols
    source_col = depart % grid_cols
    row_shift = (source_row - (face_at * elem_rows + row_index) + RY) % grid_rows
    col_shift = (source_col - (elem_at * elem_cols + col_index) + RX) % grid_cols - RX
    first = jnp.repeat(4 * (col_index + col_shift), 4, axis=1)
    which = jnp.repeat(row_shift, 4, axis=1)
    width = 2 * node_cols
    targets = []
    for n in range(4):
        col = first + n
        spot = jnp.where(col < 0, node_cols + edge + col, jnp.where(col < node_cols, col, col + edge))
        targets.append(which * width + spot)
    target = jnp.concatenate(targets, axis=1)
    weights = node_weights(offsets)
    out = pl.pallas_call(
        functools.partial(transport_kernel, elem_rows, levels),
        out_shape=jax.ShapeDtypeStruct((channels, node_rows, node_cols), jnp.float32),
        in_specs=[pl.BlockSpec(memory_space=pltpu.VMEM)] * 7,
        out_specs=pl.BlockSpec(memory_space=pltpu.VMEM),
        scratch_shapes=[
            pltpu.VMEM((elem_rows + 2, 2, 4 * channels, width), jnp.bfloat16),
            pltpu.VMEM((4, channels, 4 * node_cols), jnp.float32),
        ],
        compiler_params=pltpu.CompilerParams(vmem_limit_bytes=48 * 1024 * 1024),
        name="transport",
    )(low, rows_first, high, halo, target, weights, height.transpose(1, 0, 2))
    return (out.reshape(tracers.shape), height, new_winds)


def solution(mesh):
    in_specs = (
        P(None, None, "face", "elem"),
        P(None, "face", "elem"),
        P(None, None, "face", "elem"),
        P(),
        P("face", "elem"),
        P(None, "face", "elem"),
    )
    out_specs = (
        P(None, None, "face", "elem"),
        P(None, "face", "elem"),
        P(None, None, "face", "elem"),
    )
    return jax.shard_map(step, mesh=mesh, in_specs=in_specs, out_specs=out_specs, check_vma=False)
```

```python
import functools
import math

import jax
import jax.numpy as jnp
import numpy as np
from jax import lax
from jax.experimental import pallas as pl
from jax.experimental.pallas import tpu as pltpu
from jax.sharding import PartitionSpec as P

SUBSTEPS = 2
RX = 3
RY = 1
OFFS = 64


def gll_points():
    inner = 1.0 / math.sqrt(5.0)
    return [-1.0, -inner, inner, 1.0]


def derivative():
    points = gll_points()
    table = np.zeros((4, 4))
    for target in range(4):
        for source in range(4):
            total_value = 0.0
            for other in range(4):
                if other != source:
                    factor = 1.0 / (points[source] - points[other])
                    for fourth in range(4):
                        if fourth != source and fourth != other:
                            factor = (
                                factor
                                * (points[target] - points[fourth])
                                / (points[source] - points[fourth])
                            )
                    total_value = total_value + factor
            table[target, source] = total_value
    return table


def lagrange(coord):
    points = gll_points()
    values_list = []
    for source in range(4):
        value = jnp.ones_like(coord)
        for other in range(4):
            if other != source:
                value = value * ((coord - points[other]) / (points[source] - points[other]))
        values_list.append(value)
    return jnp.stack(values_list, axis=-1)


def roll_table():
    table = derivative()
    shifts = np.zeros((7, 4))
    for target in range(4):
        for source in range(4):
            shifts[source - target + 3, target] = table[target, source]
    return shifts


def apply_shifts(field, table, axis):
    shape = field.shape
    if axis == 1:
        field = field.reshape(-1, 8, shape[2])
        table = table[:, :8]
    size = field.shape[axis]
    total = field * table[3][None]
    for k in (-3, -2, -1, 1, 2, 3):
        total = total + pltpu.roll(field, (-k) % size, axis) * table[k + 3][None]
    return total.reshape(shape)


def selected(table, values, dim, values_first):
    table = table.astype(jnp.bfloat16)
    total = None
    rest = values
    for _ in range(3):
        piece = rest.astype(jnp.bfloat16)
        rest = rest - piece.astype(jnp.float32)
        pair = (piece, table) if values_first else (table, piece)
        term = lax.dot_general(
            *pair, (((dim,), (dim,)), ((), ())), preferred_element_type=jnp.float32
        )
        total = term if total is None else total + term
    return total


def wave_kernel(
    thickness, winds, rate, by_col, by_row, take, put, height, winds_out,
    fresh, across, side, col_send, col_recv, row_send, row_recv, send_sem, recv_sem,
):
    levels, rows, cols = thickness.shape
    chunk = 8
    neighbours = []
    for axis in ("elem", "face"):
        count = lax.axis_size(axis)
        here = lax.axis_index(axis)
        neighbours.append((axis, lax.rem(here + 1, count), lax.rem(here + count - 1, count)))
    barrier = pltpu.get_barrier_semaphore()
    for axis, up, down in neighbours:
        for place in (up, down):
            pl.semaphore_signal(
                barrier, inc=1, device_id={axis: place}, device_id_type=pl.DeviceIdType.MESH
            )
    pl.semaphore_wait(barrier, 4)

    lane = lax.broadcasted_iota(jnp.int32, (rows, cols), 1)
    line = lax.broadcasted_iota(jnp.int32, (rows, cols), 0)

    def masks(position, size):
        later = jnp.where((position % 4 == 3) & (position != size - 1), 0.5, 0.0)
        earlier = jnp.where((position % 4 == 0) & (position != 0), 0.5, 0.0)
        own = jnp.where((position % 4 == 0) | (position % 4 == 3), 0.5, 1.0)
        return own[None], later[None], earlier[None]

    def exchange(number, which, sources, targets):
        axis, up, down = neighbours[which]
        copies = []
        for way, place in ((0, up), (1, down)):
            copies.append(
                pltpu.make_async_remote_copy(
                    src_ref=sources[way],
                    dst_ref=targets[way],
                    send_sem=send_sem.at[number, which, way],
                    recv_sem=recv_sem.at[number, which, way],
                    device_id={axis: place},
                    device_id_type=pl.DeviceIdType.MESH,
                )
            )
        for copy in copies:
            copy.start()
        for copy in copies:
            copy.wait()

    def average(number, count, store):
        edges = None
        for f in range(count):
            flat = fresh[f].reshape(levels * rows, cols)
            term = selected(take[f], flat, 1, False)
            edges = term if edges is None else edges + term
        col_send[number] = edges
        exchange(
            number, 0,
            (col_send.at[number], col_send.at[number]),
            (col_recv.at[number, 0], col_recv.at[number, 1]),
        )
        both = jnp.concatenate([col_recv[number, 0], col_recv[number, 1]], axis=0)
        own, later, earlier = masks(lane, cols)
        for f in range(count):
            spread = selected(put[f], both, 0, True)
            side[f] = spread.reshape(levels, rows, cols)

            @pl.loop(0, levels // chunk)
            def _(step, f=f):
                at = pl.ds(pl.multiple_of(step * chunk, chunk), chunk)
                field = fresh[f, at]
                mixed = field * own + pltpu.roll(field, cols - 1, 2) * later
                mixed = mixed + pltpu.roll(field, 1, 2) * earlier + side[f, at]
                across[f, at] = mixed
                row_send[number, 0, f, at, :] = mixed[:, rows - 1, :]
                row_send[number, 1, f, at, :] = mixed[:, 0, :]

        exchange(
            number, 1,
            (row_send.at[number, 0, pl.ds(0, count)], row_send.at[number, 1, pl.ds(0, count)]),
            (row_recv.at[number, 0, pl.ds(0, count)], row_recv.at[number, 1, pl.ds(0, count)]),
        )
        own_row, later_row, earlier_row = masks(line, rows)
        first = jnp.where(line == 0, 0.5, 0.0)[None]
        last = jnp.where(line == rows - 1, 0.5, 0.0)[None]
        for f in range(count):

            @pl.loop(0, levels // chunk)
            def _(step, f=f):
                at = pl.ds(pl.multiple_of(step * chunk, chunk), chunk)
                field = across[f, at]
                mixed = field * own_row + pltpu.roll(field, rows - 1, 1) * later_row
                mixed = mixed + pltpu.roll(field, 1, 1) * earlier_row
                mixed = mixed + first * row_recv[number, 0, f, at, :][:, None, :]
                mixed = mixed + last * row_recv[number, 1, f, at, :][:, None, :]
                store(f, at, mixed)

    def store_height(f, at, value):
        height[at] = value

    def store_winds(f, at, value):
        winds_out[f, at] = value

    for substep in range(SUBSTEPS):
        old_height = thickness if substep == 0 else height
        old_winds = winds if substep == 0 else winds_out

        @pl.loop(0, levels // chunk)
        def _(step):
            at = pl.ds(pl.multiple_of(step * chunk, chunk), chunk)
            flow = apply_shifts(old_winds[0, at], by_col, 2) + apply_shifts(old_winds[1, at], by_row, 1)
            fresh[0, at] = old_height[at] - rate[at] * flow

        average(2 * substep, 1, store_height)

        @pl.loop(0, levels // chunk)
        def _(step):
            at = pl.ds(pl.multiple_of(step * chunk, chunk), chunk)
            now = height[at]
            fresh[0, at] = old_winds[0, at] - rate[at] * apply_shifts(now, by_col, 2)
            fresh[1, at] = old_winds[1, at] - rate[at] * apply_shifts(now, by_row, 1)

        average(2 * substep + 1, 2, store_winds)


def waves(thickness, winds, wave_coef):
    levels, rows, cols = thickness.shape
    shifts = roll_table()
    by_col = jnp.asarray(np.broadcast_to(np.tile(shifts, (1, cols // 4))[:, None, :], (7, rows, cols)), jnp.float32)
    by_row = jnp.asarray(np.broadcast_to(np.tile(shifts, (1, rows // 4))[:, :, None], (7, rows, cols)), jnp.float32)
    take = np.zeros((2, 8, cols))
    put = np.zeros((2, 16, cols))
    for f in range(2):
        take[f, 2 * f, 0] = 1.0
        take[f, 2 * f + 1, cols - 1] = 1.0
        put[f, 2 * f + 1, 0] = 0.5
        put[f, 8 + 2 * f, cols - 1] = 0.5
    rate = jnp.broadcast_to(wave_coef[:, None, None], (levels, 1, cols))
    rounds = 2 * SUBSTEPS
    wide = levels * rows
    return pl.pallas_call(
        wave_kernel,
        out_shape=(
            jax.ShapeDtypeStruct(thickness.shape, jnp.float32),
            jax.ShapeDtypeStruct(winds.shape, jnp.float32),
        ),
        in_specs=[pl.BlockSpec(memory_space=pltpu.VMEM)] * 7,
        out_specs=(pl.BlockSpec(memory_space=pltpu.VMEM), pl.BlockSpec(memory_space=pltpu.VMEM)),
        scratch_shapes=[
            pltpu.VMEM(winds.shape, jnp.float32),
            pltpu.VMEM(winds.shape, jnp.float32),
            pltpu.VMEM(winds.shape, jnp.float32),
            pltpu.VMEM((rounds, 8, wide), jnp.float32),
            pltpu.VMEM((rounds, 2, 8, wide), jnp.float32),
            pltpu.VMEM((rounds, 2, 2, levels, cols), jnp.float32),
            pltpu.VMEM((rounds, 2, 2, levels, cols), jnp.float32),
            pltpu.SemaphoreType.DMA((rounds, 2, 2)),
            pltpu.SemaphoreType.DMA((rounds, 2, 2)),
        ],
        compiler_params=pltpu.CompilerParams(
            collective_id=0, has_side_effects=True, vmem_limit_bytes=40 * 1024 * 1024
        ),
        cost_estimate=pl.CostEstimate(flops=300000000, bytes_accessed=60000000, transcendentals=0),
        name="waves",
    )(
        thickness, winds, rate, by_col, by_row,
        jnp.asarray(take, jnp.float32), jnp.asarray(put, jnp.float32),
    )


def node_weights(offsets):
    coord = -1.0 + (2.0 * offsets.astype(jnp.float32) + 1.0) / OFFS
    across = lagrange(coord[0])
    upward = lagrange(coord[1])
    weights = upward[..., :, None] * across[..., None, :]
    return weights.reshape(offsets.shape[1], offsets.shape[2], 16).transpose(2, 0, 1)


def shift_both(forward_piece, backward_piece, axis):
    count = lax.axis_size(axis)
    forward = [(i, (i + 1) % count) for i in range(count)]
    backward = [(target, source) for source, target in forward]
    return lax.ppermute(forward_piece, axis, forward), lax.ppermute(backward_piece, axis, backward)


def transport_kernel(elem_rows, levels, low, main, high, halo, target, weights, height, out, parts, picked):
    channels = main.shape[1]
    cols = main.shape[2]
    for row in range(4 * (elem_rows + 2)):
        if row < 4:
            middle = low[row]
        elif row < 4 * (elem_rows + 1):
            middle = main[row - 4]
        else:
            middle = high[row - 4 * (elem_rows + 1)]
        whole = jnp.concatenate([middle, halo[row]], axis=1)
        coarse = whole.astype(jnp.bfloat16)
        fine = (whole - coarse.astype(jnp.float32)).astype(jnp.bfloat16)
        at = pl.ds((row % 4) * channels, channels)
        parts[row // 4, 0, at, :] = coarse
        parts[row // 4, 1, at, :] = fine
    width = parts.shape[-1]
    chunk = 24
    for er in range(elem_rows):
        place = lax.broadcasted_iota(jnp.int32, (3 * width, 4 * cols), 0)
        hot = jnp.where(place == target[er : er + 1, :], 1.0, 0.0).astype(jnp.bfloat16)
        for m in range(4):
            at = pl.ds(m * channels, channels)
            total = None
            for piece in range(2):
                left = jnp.concatenate([parts[er + k, piece, at, :] for k in range(3)], axis=1)
                term = jnp.dot(left, hot, preferred_element_type=jnp.float32)
                total = term if total is None else total + term
            picked[m] = total

        @pl.loop(0, channels // chunk)
        def _(step, er=er):
            start = pl.multiple_of(step * chunk, 8)
            level = pl.multiple_of(lax.rem(step, levels // chunk) * chunk, 8)
            nodes = [
                picked[m, pl.ds(start, chunk), n * cols : (n + 1) * cols]
                for m in range(4)
                for n in range(4)
            ]
            lowest = nodes[0]
            highest = nodes[0]
            for node in nodes[1:]:
                lowest = jnp.minimum(lowest, node)
                highest = jnp.maximum(highest, node)
            for a in range(4):
                row = 4 * er + a
                value = weights[0, row : row + 1, :] * nodes[0]
                for s in range(1, 16):
                    value = value + weights[s, row : row + 1, :] * nodes[s]
                value = jnp.minimum(jnp.maximum(value, lowest), highest)
                out[pl.ds(start, chunk), row, :] = value * height[row, pl.ds(level, chunk), :]


def step(tracers, thickness, winds, wave_coef, depart, offsets):
    count, levels, node_rows, node_cols = tracers.shape
    elem_rows = node_rows // 4
    elem_cols = node_cols // 4
    channels = count * levels
    face_at = lax.axis_index("face")
    elem_at = lax.axis_index("elem")
    grid_rows = elem_rows * lax.axis_size("face")
    grid_cols = elem_cols * lax.axis_size("elem")
    rows_first = tracers.reshape(channels, node_rows, node_cols).transpose(1, 0, 2)
    edge = 4 * RX
    left, right = shift_both(
        rows_first[:, :, -edge:].transpose(0, 2, 1), rows_first[:, :, :edge].transpose(0, 2, 1), "elem"
    )
    sides = jnp.concatenate([left, right], axis=1)
    under, above = shift_both(sides[-4:], sides[:4], "face")
    sides = jnp.concatenate([under, sides, above], axis=0)
    halo = jnp.pad(sides, ((0, 0), (0, node_cols - 2 * edge), (0, 0))).transpose(0, 2, 1)
    halo, rows_first, thickness, winds = lax.optimization_barrier((halo, rows_first, thickness, winds))
    low, high = shift_both(rows_first[-4:], rows_first[:4], "face")
    height, new_winds = waves(thickness, winds, wave_coef)

    row_index = lax.broadcasted_iota(jnp.int32, (elem_rows, elem_cols), 0)
    col_index = lax.broadcasted_iota(jnp.int32, (elem_rows, elem_cols), 1)
    source_row = depart // grid_cols
    source_col = depart % grid_cols
    row_shift = (source_row - (face_at * elem_rows + row_index) + RY) % grid_rows
    col_shift = (source_col - (elem_at * elem_cols + col_index) + RX) % grid_cols - RX
    first = jnp.repeat(4 * (col_index + col_shift), 4, axis=1)
    which = jnp.repeat(row_shift, 4, axis=1)
    width = 2 * node_cols
    targets = []
    for n in range(4):
        col = first + n
        spot = jnp.where(col < 0, node_cols + edge + col, jnp.where(col < node_cols, col, col + edge))
        targets.append(which * width + spot)
    target = jnp.concatenate(targets, axis=1)
    weights = node_weights(offsets)
    out = pl.pallas_call(
        functools.partial(transport_kernel, elem_rows, levels),
        out_shape=jax.ShapeDtypeStruct((channels, node_rows, node_cols), jnp.float32),
        in_specs=[pl.BlockSpec(memory_space=pltpu.VMEM)] * 7,
        out_specs=pl.BlockSpec(memory_space=pltpu.VMEM),
        scratch_shapes=[
            pltpu.VMEM((elem_rows + 2, 2, 4 * channels, width), jnp.bfloat16),
            pltpu.VMEM((4, channels, 4 * node_cols), jnp.float32),
        ],
        compiler_params=pltpu.CompilerParams(vmem_limit_bytes=48 * 1024 * 1024),
        name="transport",
    )(low, rows_first, high, halo, target, weights, height.transpose(1, 0, 2))
    return (out.reshape(tracers.shape), height, new_winds)


def solution(mesh):
    in_specs = (
        P(None, None, "face", "elem"),
        P(None, "face", "elem"),
        P(None, None, "face", "elem"),
        P(),
        P("face", "elem"),
        P(None, "face", "elem"),
    )
    out_specs = (
        P(None, None, "face", "elem"),
        P(None, "face", "elem"),
        P(None, None, "face", "elem"),
    )
    return jax.shard_map(step, mesh=mesh, in_specs=in_specs, out_specs=out_specs, check_vma=False)
```
